32 devices in a mesh: layer: 8 (over y, x, core), dp: 4 (over z).
Axes of the slice: x: 2, y: 2, z: 4, core: 2. Of those that a mesh axis runs over, the one named last changes fastest.
Arguments:
- states: bfloat16 [64, 8, 64, 256], P('layer', 'dp'), may hold values from -6 to 6
- kernels: bfloat16 [64, 9, 64, 64], P('layer'), may hold values from -0.25 to 0.25
- boundary: float32 [8, 8, 64, 256], P('layer', 'dp'), may hold values from -6 to 6
Outputs:
- corrected: float32 [8, 8, 64, 256], P('layer', 'dp')
- bottoms: float32 [8, 8, 64, 256], P('layer', 'dp')
- gradients: float32 [64, 9, 64, 64], P('layer')
The draws below stay inside these ranges and needn't reach their ends.
All inputs are finite; a program needn't handle non-finite values.
Results may differ from the reference program's by a relative error of at most 0.012.
Values may be sent and summed in bfloat16 or wider, within the bound.
A program may use at most 64 MiB of HBM per device.

```python
import jax
import jax.numpy as jnp
from jax import lax

CH = 64
MAP = 16
LD = 8
BLOCKS = 8
LAYERS = 64
BATCH = 8


def level_of(rng, extent, shards, smallest, largest):
    loudness, own = 1.0, jax.random.fold_in(rng, 6)
    for dim, blocks in shards:
        draws = jnp.exp(jax.random.uniform(jax.random.fold_in(own, dim), (blocks,), jnp.float32, smallest / len(shards), largest / len(shards)))
        loudness = loudness * jnp.repeat(draws, extent[dim] // blocks).reshape([-1 if axis == dim else 1 for axis in range(len(extent))])
    return loudness


def scatter_about(stream_key, shape, deviation, reach, shards=(), held_as=jnp.bfloat16):
    gain = level_of(stream_key, shape, shards, -0.22, 0.18) if shards else 1.0
    values = jax.random.normal(stream_key, shape, jnp.float32) * deviation * gain
    return jnp.minimum(jnp.maximum(values, -reach), reach).astype(held_as)


def setup_inputs(seed: int = 0) -> dict:
    streams_of = jax.random.split(jax.random.key(seed), 4)
    return {
        "states": scatter_about(streams_of[0], (LAYERS, BATCH, CH, MAP * MAP), 1.0, 6.0, ((0, 8), (1, 4))),
        "kernels": scatter_about(streams_of[1], (LAYERS, 9, CH, CH), (9 * CH) ** -0.5, 0.25, ((0, 8),)),
        "boundary": scatter_about(streams_of[2], (BLOCKS, BATCH, CH, MAP * MAP), 1.0, 6.0, ((0, 8), (1, 4)), jnp.float32),
    }


tap_offsets = [(row_shift, col_shift) for row_shift in (-1, 0, 1) for col_shift in (-1, 0, 1)]


def shifted(values, row_shift, col_shift):
    cells = MAP * MAP
    margin = MAP + 1
    widths = [(0, 0)] * (values.ndim - 1) + [(margin, margin)]
    padded = jnp.pad(values, widths)
    start = margin - (row_shift * MAP + col_shift)
    moved = padded[..., start:start + cells]
    column = jnp.arange(cells, dtype=jnp.int32) % MAP - col_shift
    keep = (column >= 0) & (column < MAP)
    return jnp.where(keep, moved, jnp.zeros((), values.dtype))


def stacked(values, direction):
    return jnp.stack([shifted(values, direction * row_shift, direction * col_shift) for row_shift, col_shift in tap_offsets], axis=1)


def rounded(values):
    return lax.optimization_barrier(values.astype(jnp.bfloat16))


def adjoint_conv(kernel, rounded_adj):
    taps = stacked(rounded_adj, 1).astype(jnp.float32)
    return jnp.einsum("toc,btoh->bch", kernel.astype(jnp.float32), taps)


def weight_terms(rounded_adj, activation):
    taps = stacked(activation, -1).astype(jnp.float32)
    return jnp.einsum("boh,btch->toc", rounded_adj.astype(jnp.float32), taps)


def coarse_step(adjoint, kernel_mean):
    return adjoint + 0.5 * adjoint_conv(kernel_mean, rounded(adjoint))


def sweep_block(upper_value, block_states, block_kernels, keep_grads):
    step_size = 0.5 / LD
    collected = []
    for layer_pos in reversed(range(LD)):
        rounded_adj = rounded(upper_value)
        hyperbolic = jnp.tanh(block_states[layer_pos].astype(jnp.float32))
        slope = 1.0 - hyperbolic * hyperbolic
        if keep_grads:
            collected.append(weight_terms(rounded_adj, rounded(hyperbolic)) * (step_size / BATCH))
        upper_value = upper_value + step_size * slope * adjoint_conv(block_kernels[layer_pos], rounded_adj)
    if keep_grads:
        return upper_value, jnp.stack(collected[::-1], axis=0)
    return upper_value


def reference(states, kernels, boundary):
    block_states = states.reshape(BLOCKS, LD, BATCH, CH, MAP * MAP)
    block_kernels = kernels.reshape(BLOCKS, LD, 9, CH, CH)

    def first_pass(pieces):
        return sweep_block(pieces[0], pieces[1], pieces[2], False)

    first_bottoms = lax.map(first_pass, (boundary, block_states, block_kernels))
    kernel_means = rounded(jnp.mean(block_kernels.astype(jnp.float32), axis=1))

    def coarse_source(pieces):
        return pieces[0] - coarse_step(pieces[1], pieces[2])

    sources = lax.map(coarse_source, (first_bottoms, boundary, kernel_means))

    def backward(carried, pieces):
        updated = coarse_step(carried, pieces[0]) + pieces[1]
        return updated, updated

    final_carry, earlier = lax.scan(backward, boundary[-1], (kernel_means[1:], sources[1:]), reverse=True)
    corrected = jnp.concatenate([earlier, boundary[-1:]], axis=0)

    def last_pass(pieces):
        return sweep_block(pieces[0], pieces[1], pieces[2], True)

    new_bottoms, gradients = lax.map(last_pass, (corrected, block_states, block_kernels))
    return corrected, new_bottoms, gradients.reshape(LAYERS, 9, CH, CH)
```

```python
import functools

import jax
import jax.numpy as jnp
from jax import lax
from jax.experimental import pallas as pl
from jax.experimental.pallas import tpu as pltpu
from jax.sharding import PartitionSpec as P

MAP = 16
CELLS = MAP * MAP
LD = 8
CH = 64
STEP = 0.5 / LD
MESH_ID = pl.DeviceIdType.MESH
f32, bf16 = jnp.float32, jnp.bfloat16


def kernel(blocks, parts, samples, states_in, kernels_in, boundary_in, corrected, bottoms, grads,
           states, kernels, boundary, in_sem, weights, slopes, acts, act_rows, mean_own, means, src_own, srcs,
           adj, chain, swap_out, swap_in, own, from_outer, half, from_across, whole, from_inner,
           mean_send, mean_recv, fwd_send, src_send, src_recv, swap_send, swap_recv,
           a_send, a_recv, b_send, b_recv, c_send, c_recv):
    me = lax.axis_index("layer")
    dp = lax.axis_index("dp")
    lanes = samples * CELLS
    width = lanes // 2
    core = lax.rem(me, 2)
    base = me - core
    other = me + 1 - 2 * core
    last = base == blocks - 2

    barrier = pltpu.get_barrier_semaphore()
    for i in range(1, blocks):
        pl.semaphore_signal(barrier, inc=1, device_id=(lax.rem(me + i, blocks), dp), device_id_type=MESH_ID)
    for i in range(1, parts):
        pl.semaphore_signal(barrier, inc=1, device_id=(me, lax.rem(dp + i, parts)), device_id_type=MESH_ID)

    loads = [pltpu.make_async_copy(kernels_in, kernels, in_sem.at[0]),
             pltpu.make_async_copy(boundary_in, boundary, in_sem.at[1]),
             pltpu.make_async_copy(states_in, states, in_sem.at[2])]
    for load in loads:
        load.start()

    cell = lax.broadcasted_iota(jnp.int32, (CH, lanes), 1)
    col = lax.bitwise_and(cell, MAP - 1)
    row = lax.bitwise_and(lax.shift_right_logical(cell, 4), MAP - 1)
    col_lo, col_hi = col >= 1, col <= MAP - 2
    row_lo, row_hi = row >= 1, row <= MAP - 2

    def cols(v):
        size = v.shape[1]
        left = jnp.where(col_hi[:, :size], pltpu.roll(v, size - 1, 1), 0.0)
        right = jnp.where(col_lo[:, :size], pltpu.roll(v, 1, 1), 0.0)
        return jnp.concatenate([left.astype(bf16), v.astype(bf16), right.astype(bf16)], axis=0)

    def rows_up(v):
        return jnp.where(row_hi[:, :v.shape[1]], pltpu.roll(v, v.shape[1] - MAP, 1), 0.0)

    def rows_down(v):
        return jnp.where(row_lo[:, :v.shape[1]], pltpu.roll(v, MAP, 1), 0.0)

    def conv(w, v):
        r = jnp.dot(w, v, preferred_element_type=f32)
        return rows_up(r[:CH]) + r[CH:2 * CH] + rows_down(r[2 * CH:])

    def flat(ref):
        return jnp.concatenate([ref[n] for n in range(samples)], axis=1)

    def turned(ks):
        return jnp.concatenate([k.astype(f32) for k in ks], axis=1).T.astype(bf16)

    loads[0].wait()
    total = [kernels[0, a].astype(f32) for a in range(3)]
    for l in range(1, LD):
        for a in range(3):
            total[a] = total[a] + kernels[l, a].astype(f32)
    mean = turned([t * (1.0 / LD) for t in total])
    mean_own[:3 * CH] = mean[:, :2 * CH]
    mean_own[3 * CH:] = jnp.concatenate([mean[:3 * CH // 2, 2 * CH:], mean[3 * CH // 2:, 2 * CH:]], axis=1)

    def unpacked(m):
        tail = jnp.concatenate([m[3 * CH:, :CH], m[3 * CH:, CH:]], axis=0)
        return jnp.concatenate([m[:3 * CH], tail], axis=1)

    pl.semaphore_wait(barrier, blocks - 1 + parts - 1)

    def mean_copy(peer):
        return pltpu.make_async_remote_copy(
            src_ref=mean_own, dst_ref=means.at[me], send_sem=mean_send.at[peer],
            recv_sem=mean_recv.at[me], device_id=(peer, dp), device_id_type=MESH_ID)

    def src_copy(peer, part):
        return pltpu.make_async_remote_copy(
            src_ref=src_own.at[part], dst_ref=srcs.at[me], send_sem=src_send.at[peer],
            recv_sem=src_recv.at[me], device_id=(peer, dp), device_id_type=MESH_ID)

    def mean_arrival(j):
        return pltpu.make_async_remote_copy(
            src_ref=mean_own, dst_ref=means.at[j], send_sem=mean_send.at[0],
            recv_sem=mean_recv.at[j], device_id=(other, dp), device_id_type=MESH_ID)

    def src_arrival(j):
        return pltpu.make_async_remote_copy(
            src_ref=src_own.at[0], dst_ref=srcs.at[j], send_sem=src_send.at[0],
            recv_sem=src_recv.at[j], device_id=(other, dp), device_id_type=MESH_ID)

    swap = pltpu.make_async_remote_copy(
        src_ref=swap_out, dst_ref=swap_in, send_sem=swap_send, recv_sem=swap_recv,
        device_id=(other, dp), device_id_type=MESH_ID)

    def forward(j):
        return pltpu.make_async_remote_copy(
            src_ref=means.at[j], dst_ref=means.at[j], send_sem=fwd_send.at[j],
            recv_sem=mean_recv.at[j], device_id=(other, dp), device_id_type=MESH_ID)

    for lower in range(0, blocks - 2, 2):
        @pl.when(jnp.logical_and(base > lower, me < blocks - 1))
        def _():
            mean_copy(lower + core).start()

    @pl.when(jnp.logical_and(core == 1, me < blocks - 1))
    def _():
        mean_copy(me - 1).start()

    loads[1].wait()
    loads[2].wait()
    top = flat(boundary.at[0])
    p = top
    for l in reversed(range(LD)):
        weights[l] = turned([kernels[l, a] for a in range(3)])
        h = jnp.tanh(flat(states.at[l]).astype(f32))
        slope = STEP * (1.0 - h * h)
        acts[l] = h.astype(bf16)
        slopes[l] = slope
        p = p + slope * conv(weights[l], cols(p))
    coarse = top + 0.5 * conv(mean, cols(top))
    source = p - jnp.where(me == blocks - 1, 0.0, coarse)
    for part in range(2):
        src_own[part] = source[:, part * width:(part + 1) * width].astype(bf16)

    @pl.when(core == 1)
    def _():
        src_copy(me - 1, 0).start()

    for peer in range(blocks - 2):
        @pl.when(base > peer)
        def _():
            src_copy(peer, peer % 2).start()

    @pl.when(jnp.logical_and(last, core == 1))
    def _():
        swap_out[...] = source[:, width:]
        swap.start()

    for j in reversed(range(2, blocks - 1)):
        @pl.when(jnp.logical_and(base + 1 < j, core == j % 2))
        def _():
            mean_arrival(j).wait_recv()
            forward(j).start()

    for l in range(LD):
        h = acts[l].astype(f32)
        act_rows[l] = jnp.concatenate(
            [rows_down(h).astype(bf16), h.astype(bf16), rows_up(h).astype(bf16)], axis=0)

    @pl.when(last)
    def _():
        @pl.when(core == 1)
        def _():
            adj[...] = top

        @pl.when(core == 0)
        def _():
            src_arrival(blocks - 1).wait_recv()
            adj[:, :width] = srcs[blocks - 1].astype(f32)
            swap.wait_recv()
            adj[:, width:] = swap_in[...]

    @pl.when(jnp.logical_not(last))
    def _():
        src_arrival(blocks - 1).wait_recv()
        chain[...] = srcs[blocks - 1].astype(f32)

    for j in reversed(range(2, blocks - 1)):
        @pl.when(jnp.logical_and(base + 1 < j, core != j % 2))
        def _():
            mean_arrival(j).wait_recv()

        @pl.when(base + 1 < j)
        def _():
            e = chain[...]
            e = e + 0.5 * conv(unpacked(means[j]), cols(e))
            src_arrival(j).wait_recv()
            chain[...] = e + srcs[j].astype(f32)

    @pl.when(jnp.logical_and(jnp.logical_not(last), core == 0))
    def _():
        e = chain[...]
        swap_out[...] = e
        swap.start()
        mean_arrival(me + 1).wait_recv()
        src_arrival(me + 1).wait_recv()
        adj[:, :width] = e + 0.5 * conv(unpacked(means[me + 1]), cols(e)) + srcs[me + 1].astype(f32)
        swap.wait_recv()
        adj[:, width:] = swap_in[...]

    @pl.when(jnp.logical_and(jnp.logical_not(last), core == 1))
    def _():
        e = chain[...]
        swap_out[...] = e + 0.5 * conv(unpacked(mean_own[...]), cols(e)) + src_own[1].astype(f32)
        swap.start()
        adj[:, width:] = e
        swap.wait_recv()
        adj[:, :width] = swap_in[...]

    p = adj[...]
    for n in range(samples):
        corrected[0, n] = p[:, n * CELLS:(n + 1) * CELLS]

    scale = STEP / (samples * parts)
    chunks = 3 * LD // 2
    inner = jnp.logical_or(dp == 1, dp == 2)
    outer = jnp.logical_or(dp == 0, dp == 3)
    mate = dp + 1 - 2 * lax.rem(dp, 2)
    across = 3 - dp

    def hop(src, dst, send, recv, c, peer):
        return pltpu.make_async_remote_copy(
            src_ref=src.at[c], dst_ref=dst.at[c], send_sem=send.at[c], recv_sem=recv.at[c],
            device_id=(me, peer), device_id_type=MESH_ID)

    def to_inner(c):
        return hop(own, from_outer, a_send, a_recv, c, mate)

    def to_across(c):
        return hop(half, from_across, b_send, b_recv, c, across)

    def to_outer(c):
        return hop(whole, from_inner, c_send, c_recv, c, mate)

    def put(c, v):
        g, k = c // 3, c % 3
        l = LD - 1 - 2 * g
        v = v.astype(f32)
        if k < 2:
            grads[l - k, 0] = v[:, :CH]
            grads[l - k, 1] = v[:, CH:]
        else:
            grads[l, 2] = v[:, :CH]
            grads[l - 1, 2] = v[:, CH:]

    def pair_sum(c):
        to_inner(c).wait_recv()
        half[c] = (own[c].astype(f32) + from_outer[c].astype(f32)).astype(bf16)
        to_across(c).start()

    def full_sum(c):
        to_across(c).wait_recv()
        v = (half[c].astype(f32) + from_across[c].astype(f32)).astype(bf16)
        whole[c] = v
        to_outer(c).start()
        put(c, v)

    paired, summed = 0, 0
    for i in range(LD):
        l = LD - 1 - i
        v = cols(p)
        p = p + slopes[l] * conv(weights[l], v)
        t = lax.dot_general(v, act_rows[l], (((1,), (1,)), ((), ())), preferred_element_type=f32) * scale
        c = 3 * (i // 2) + i % 2
        own[c] = t[:, :2 * CH].astype(bf16)
        ready = [c]
        if i % 2 == 0:
            kept = t[:, 2 * CH:]
        else:
            own[c + 1] = jnp.concatenate([kept, t[:, 2 * CH:]], axis=1).astype(bf16)
            ready.append(c + 1)

        @pl.when(outer)
        def _():
            for r in ready:
                to_inner(r).start()

        if i >= 2:
            @pl.when(inner)
            def _():
                pair_sum(i - 2)
                if i >= 4:
                    full_sum(i - 4)
    for n in range(samples):
        bottoms[0, n] = p[:, n * CELLS:(n + 1) * CELLS]

    @pl.when(inner)
    def _():
        for c in range(LD - 2, chunks):
            pair_sum(c)
            full_sum(c - 2)
        for c in range(chunks - 2, chunks):
            full_sum(c)
        for c in range(chunks):
            to_across(c).wait_send()
            to_outer(c).wait_send()

    @pl.when(outer)
    def _():
        for c in range(chunks):
            to_outer(c).wait_recv()
            put(c, from_inner[c])
        for c in range(chunks):
            to_inner(c).wait_send()

    for lower in range(0, blocks - 2, 2):
        @pl.when(jnp.logical_and(base > lower, me < blocks - 1))
        def _():
            mean_copy(lower + core).wait_send()

    @pl.when(jnp.logical_and(core == 1, me < blocks - 1))
    def _():
        mean_copy(me - 1).wait_send()

    for j in range(2, blocks - 1):
        @pl.when(jnp.logical_and(base + 1 < j, core == j % 2))
        def _():
            forward(j).wait_send()

    for peer in range(blocks - 2):
        @pl.when(base > peer)
        def _():
            src_copy(peer, peer % 2).wait_send()

    @pl.when(core == 1)
    def _():
        src_copy(me - 1, 0).wait_send()

    @pl.when(jnp.logical_or(jnp.logical_not(last), core == 1))
    def _():
        swap.wait_send()


def write(corrected, bottoms, grads, corrected_out, bottoms_out, grads_out, sem):
    stores = [pltpu.make_async_copy(grads, grads_out, sem.at[0]),
              pltpu.make_async_copy(corrected, corrected_out, sem.at[1]),
              pltpu.make_async_copy(bottoms, bottoms_out, sem.at[2])]
    for store in stores:
        store.start()
    for store in stores:
        store.wait()


def body(blocks, parts, states, kernels, boundary):
    samples = states.shape[1]
    lanes = samples * CELLS
    chunks = 3 * LD // 2
    vmem = pl.BlockSpec(memory_space=pltpu.VMEM)
    hbm = pl.BlockSpec(memory_space=pltpu.HBM)
    dma = pltpu.SemaphoreType.DMA
    corrected, bottoms, grads = pl.pallas_call(
        functools.partial(kernel, blocks, parts, samples),
        out_shape=(
            jax.ShapeDtypeStruct(boundary.shape, f32),
            jax.ShapeDtypeStruct(boundary.shape, f32),
            jax.ShapeDtypeStruct((LD, 3, 3 * CH, CH), f32),
        ),
        in_specs=[hbm] * 3,
        out_specs=(vmem,) * 3,
        scratch_shapes=[
            pltpu.VMEM(states.shape, bf16),
            pltpu.VMEM((LD, 3, 3 * CH, CH), bf16),
            pltpu.VMEM(boundary.shape, f32),
            dma((3,)),
            pltpu.VMEM((LD, 3 * CH, 3 * CH), bf16),
            pltpu.VMEM((LD, CH, lanes), f32),
            pltpu.VMEM((LD, CH, lanes), bf16),
            pltpu.VMEM((LD, 3 * CH, lanes), bf16),
            pltpu.VMEM((9 * CH // 2, 2 * CH), bf16),
            pltpu.VMEM((blocks, 9 * CH // 2, 2 * CH), bf16),
            pltpu.VMEM((2, CH, lanes // 2), bf16),
            pltpu.VMEM((blocks, CH, lanes // 2), bf16),
            pltpu.VMEM((CH, lanes), f32),
            *[pltpu.VMEM((CH, lanes // 2), f32)] * 3,
            *[pltpu.VMEM((chunks, 3 * CH, 2 * CH), bf16)] * 6,
            *[dma((blocks,))] * 5, dma, dma,
            *[dma((chunks,))] * 6,
        ],
        compiler_params=pltpu.CompilerParams(
            collective_id=0, has_side_effects=True, vmem_limit_bytes=40 * 1024 * 1024),
        cost_estimate=pl.CostEstimate(flops=2 * 10**9, bytes_accessed=6 * 10**6, transcendentals=262144),
        name="cycle",
    )(*[pltpu.with_memory_space_constraint(a, pltpu.HBM) for a in (states, kernels.reshape(LD, 3, 3 * CH, CH), boundary)])
    shapes = (corrected, bottoms, grads)
    corrected, bottoms, grads = pl.pallas_call(
        write,
        out_shape=tuple(jax.ShapeDtypeStruct(a.shape, a.dtype) for a in shapes),
        in_specs=[pl.BlockSpec(memory_space=pl.ANY)] * 3,
        out_specs=(hbm,) * 3,
        scratch_shapes=[dma((3,))],
        cost_estimate=pl.CostEstimate(flops=0, bytes_accessed=5 * 10**6, transcendentals=0),
        compiler_params=pltpu.CompilerParams(vmem_limit_bytes=4 * 1024 * 1024),
        name="write",
    )(*[pltpu.with_memory_space_constraint(a, pltpu.VMEM) for a in shapes])
    return corrected, bottoms, grads.reshape(LD, 9, CH, CH)


def solution(mesh):
    placed = (
        P("layer", "dp", None, None),
        P("layer", None, None, None),
        P("layer", "dp", None, None),
    )
    return jax.shard_map(
        functools.partial(body, mesh.shape["layer"], mesh.shape["dp"]),
        mesh=mesh,
        in_specs=placed,
        out_specs=(
            P("layer", "dp", None, None),
            P("layer", "dp", None, None),
            P("layer", None, None, None),
        ),
        check_vma=False,
    )
```

```python
import functools

import jax
import jax.numpy as jnp
from jax import lax
from jax.experimental import pallas as pl
from jax.experimental.pallas import tpu as pltpu
from jax.sharding import PartitionSpec as P

MAP = 16
CELLS = MAP * MAP
LD = 8
CH = 64
STEP = 0.5 / LD
M = 3
PIECES = 1
PACKED = 9 * CH // 2
PIECE = PACKED // PIECES
MESH_ID = pl.DeviceIdType.MESH
f32, bf16 = jnp.float32, jnp.bfloat16


def kernel(blocks, parts, samples, states_in, kernels_in, boundary_in, corrected, bottoms, grads,
           states, kernels, boundary, in_sem, weights, slopes, acts, act_rows, mean_own, means, src_own, srcs,
           adj, chain, swap_out, swap_in, far, adjs, rep, own, from_outer, half, from_across, whole, from_inner,
           far_send, far_recv, adj_send, adj_recv, mean_send, mean_recv, fwd_send, src_send, src_recv, swap_send, swap_recv,
           a_send, a_recv, b_send, b_recv, c_send, c_recv):
    me = lax.axis_index("layer")
    dp = lax.axis_index("dp")
    lanes = samples * CELLS
    width = lanes // 2
    core = lax.rem(me, 2)
    base = me - core
    other = me + 1 - 2 * core
    last = base == blocks - 2
    inner = jnp.logical_or(dp == 1, dp == 2)
    outer = jnp.logical_or(dp == 0, dp == 3)
    mate = dp + 1 - 2 * lax.rem(dp, 2)
    across = 3 - dp
    near = lax.div(dp, 2)

    barrier = pltpu.get_barrier_semaphore()
    for i in range(1, blocks):
        pl.semaphore_signal(barrier, inc=1, device_id=(lax.rem(me + i, blocks), dp), device_id_type=MESH_ID)
    for i in range(1, parts):
        pl.semaphore_signal(barrier, inc=1, device_id=(me, lax.rem(dp + i, parts)), device_id_type=MESH_ID)

    loads = [pltpu.make_async_copy(kernels_in, kernels, in_sem.at[0]),
             pltpu.make_async_copy(boundary_in, boundary, in_sem.at[1]),
             pltpu.make_async_copy(states_in, states, in_sem.at[2])]
    for load in loads:
        load.start()

    cell = lax.broadcasted_iota(jnp.int32, (CH, 2 * lanes), 1)
    col = lax.bitwise_and(cell, MAP - 1)
    row = lax.bitwise_and(lax.shift_right_logical(cell, 4), MAP - 1)
    col_lo, col_hi = col >= 1, col <= MAP - 2
    row_lo, row_hi = row >= 1, row <= MAP - 2

    def cols(v):
        size = v.shape[1]
        left = jnp.where(col_hi[:, :size], pltpu.roll(v, size - 1, 1), 0.0)
        right = jnp.where(col_lo[:, :size], pltpu.roll(v, 1, 1), 0.0)
        return jnp.concatenate([left.astype(bf16), v.astype(bf16), right.astype(bf16)], axis=0)

    def rows_up(v):
        return jnp.where(row_hi[:, :v.shape[1]], pltpu.roll(v, v.shape[1] - MAP, 1), 0.0)

    def rows_down(v):
        return jnp.where(row_lo[:, :v.shape[1]], pltpu.roll(v, MAP, 1), 0.0)

    def conv(w, v):
        r = jnp.dot(w, v, preferred_element_type=f32)
        return rows_up(r[:CH]) + r[CH:2 * CH] + rows_down(r[2 * CH:])

    def flat(ref):
        return jnp.concatenate([ref[n] for n in range(samples)], axis=1)

    def turned(ks):
        return jnp.concatenate([k.astype(f32) for k in ks], axis=1).T.astype(bf16)

    loads[0].wait()
    total = [kernels[0, a].astype(f32) for a in range(3)]
    for l in range(1, LD):
        for a in range(3):
            total[a] = total[a] + kernels[l, a].astype(f32)
    mean = turned([t * (1.0 / LD) for t in total])
    mean_own[:3 * CH] = mean[:, :2 * CH]
    mean_own[3 * CH:] = jnp.concatenate([mean[:3 * CH // 2, 2 * CH:], mean[3 * CH // 2:, 2 * CH:]], axis=1)

    def unpacked(m):
        tail = jnp.concatenate([m[3 * CH:, :CH], m[3 * CH:, CH:]], axis=0)
        return jnp.concatenate([m[:3 * CH], tail], axis=1)

    pl.semaphore_wait(barrier, blocks - 1 + parts - 1)

    def mean_copy(peer):
        return pltpu.make_async_remote_copy(
            src_ref=mean_own, dst_ref=means.at[me], send_sem=mean_send.at[peer],
            recv_sem=mean_recv.at[me], device_id=(peer, dp), device_id_type=MESH_ID)

    def src_copy(peer, part):
        return pltpu.make_async_remote_copy(
            src_ref=src_own.at[part], dst_ref=srcs.at[me], send_sem=src_send.at[peer],
            recv_sem=src_recv.at[me], device_id=(peer, dp), device_id_type=MESH_ID)

    def mean_arrival(j):
        return pltpu.make_async_remote_copy(
            src_ref=mean_own, dst_ref=means.at[j], send_sem=mean_send.at[0],
            recv_sem=mean_recv.at[j], device_id=(other, dp), device_id_type=MESH_ID)

    def src_arrival(j):
        return pltpu.make_async_remote_copy(
            src_ref=src_own.at[0], dst_ref=srcs.at[j], send_sem=src_send.at[0],
            recv_sem=src_recv.at[j], device_id=(other, dp), device_id_type=MESH_ID)

    def far_copy(src, s, i, n, peer):
        return pltpu.make_async_remote_copy(
            src_ref=src, dst_ref=far.at[s, i], send_sem=far_send.at[n, i], recv_sem=far_recv.at[s, i],
            device_id=(me, peer), device_id_type=MESH_ID)

    def far_sends(i):
        src = states.at[LD - 1 - i]
        return far_copy(src, dp, i, 0, 2 - near), far_copy(src, dp, i, 1, mate)

    def far_forward(i, n):
        s = across if n == 2 else 3 - mate
        return far_copy(far.at[s, i], s, i, n, mate)

    def far_arrival(s, i):
        return far_copy(far.at[s, i], s, i, 0, mate)

    def adj_copy(s, n, peer):
        return pltpu.make_async_remote_copy(
            src_ref=adjs.at[s], dst_ref=adjs.at[s], send_sem=adj_send.at[n], recv_sem=adj_recv.at[s],
            device_id=(me, peer), device_id_type=MESH_ID)

    def adj_to_mate():
        return adj_copy(dp, 0, mate)

    def adj_to_across():
        return adj_copy(dp, 1, across)

    def adj_forwards():
        return adj_copy(mate, 2, across), adj_copy(across, 3, mate), adj_copy(3 - mate, 4, mate)

    forwards = [(i, n) for i in range(M) for n in (2, 3)]

    def pass_on(count):
        for i, n in forwards[:count]:
            @pl.when(inner)
            def _():
                far_arrival(across if n == 2 else 3 - mate, i).wait_recv()
                far_forward(i, n).start()
        del forwards[:count]

    swap = pltpu.make_async_remote_copy(
        src_ref=swap_out, dst_ref=swap_in, send_sem=swap_send, recv_sem=swap_recv,
        device_id=(other, dp), device_id_type=MESH_ID)

    def forward(j):
        return pltpu.make_async_remote_copy(
            src_ref=means.at[j], dst_ref=means.at[j], send_sem=fwd_send.at[j],
            recv_sem=mean_recv.at[j], device_id=(other, dp), device_id_type=MESH_ID)

    for lower in range(0, blocks - 2, 2):
        @pl.when(jnp.logical_and(base > lower, me < blocks - 1))
        def _():
            mean_copy(lower + core).start()

    @pl.when(jnp.logical_and(core == 1, me < blocks - 1))
    def _():
        mean_copy(me - 1).start()

    loads[2].wait()
    for i in range(M):
        for copy in far_sends(i):
            copy.start()
        far[dp, i] = states[LD - 1 - i]

    loads[1].wait()
    top = flat(boundary.at[0])
    p = top
    for l in reversed(range(LD)):
        weights[l] = turned([kernels[l, a] for a in range(3)])
        h = jnp.tanh(flat(states.at[l]).astype(f32))
        slope = STEP * (1.0 - h * h)
        acts[l] = h.astype(bf16)
        slopes[l] = slope
        p = p + slope * conv(weights[l], cols(p))
    coarse = top + 0.5 * conv(mean, cols(top))
    source = p - jnp.where(me == blocks - 1, 0.0, coarse)
    for part in range(2):
        src_own[part] = source[:, part * width:(part + 1) * width].astype(bf16)

    @pl.when(core == 1)
    def _():
        src_copy(me - 1, 0).start()

    for peer in range(blocks - 2):
        @pl.when(base > peer)
        def _():
            src_copy(peer, peer % 2).start()

    @pl.when(jnp.logical_and(last, core == 1))
    def _():
        swap_out[...] = source[:, width:]
        swap.start()

    for j in reversed(range(2, blocks - 1)):
        @pl.when(jnp.logical_and(base + 1 < j, core == j % 2))
        def _():
            mean_arrival(j).wait_recv()
            forward(j).start()

    pass_on(1)
    for l in range(LD - M):
        h = acts[l].astype(f32)
        act_rows[l] = jnp.concatenate(
            [rows_down(h).astype(bf16), h.astype(bf16), rows_up(h).astype(bf16)], axis=0)

    @pl.when(last)
    def _():
        @pl.when(core == 1)
        def _():
            adj[...] = top

        @pl.when(core == 0)
        def _():
            src_arrival(blocks - 1).wait_recv()
            adj[:, :width] = srcs[blocks - 1].astype(f32)
            swap.wait_recv()
            adj[:, width:] = swap_in[...]

    @pl.when(jnp.logical_not(last))
    def _():
        src_arrival(blocks - 1).wait_recv()
        chain[...] = srcs[blocks - 1].astype(f32)

    for j in reversed(range(2, blocks - 1)):
        pass_on(1)

        @pl.when(jnp.logical_and(base + 1 < j, core != j % 2))
        def _():
            mean_arrival(j).wait_recv()

        @pl.when(base + 1 < j)
        def _():
            e = chain[...]
            e = e + 0.5 * conv(unpacked(means[j]), cols(e))
            src_arrival(j).wait_recv()
            chain[...] = e + srcs[j].astype(f32)

    @pl.when(jnp.logical_and(jnp.logical_not(last), core == 0))
    def _():
        e = chain[...]
        swap_out[...] = e
        swap.start()
        mean_arrival(me + 1).wait_recv()
        src_arrival(me + 1).wait_recv()
        adj[:, :width] = e + 0.5 * conv(unpacked(means[me + 1]), cols(e)) + srcs[me + 1].astype(f32)
        swap.wait_recv()
        adj[:, width:] = swap_in[...]

    @pl.when(jnp.logical_and(jnp.logical_not(last), core == 1))
    def _():
        e = chain[...]
        swap_out[...] = e + 0.5 * conv(unpacked(mean_own[...]), cols(e)) + src_own[1].astype(f32)
        swap.start()
        adj[:, width:] = e
        swap.wait_recv()
        adj[:, :width] = swap_in[...]

    p = adj[...]
    adjs[dp] = p.astype(bf16)
    adj_to_mate().start()

    @pl.when(inner)
    def _():
        adj_to_across().start()

    for n in range(samples):
        corrected[0, n] = p[:, n * CELLS:(n + 1) * CELLS]

    scale = STEP / (samples * parts)
    chunks = (LD - M) * PIECES

    def hop(src, dst, send, recv, c, peer):
        part = (c // PIECES, pl.ds(c % PIECES * PIECE, PIECE))
        return pltpu.make_async_remote_copy(
            src_ref=src.at[part], dst_ref=dst.at[part], send_sem=send.at[c], recv_sem=recv.at[c],
            device_id=(me, peer), device_id_type=MESH_ID)

    def to_inner(c):
        return hop(own, from_outer, a_send, a_recv, c, mate)

    def to_across(c):
        return hop(half, from_across, b_send, b_recv, c, across)

    def to_outer(c):
        return hop(whole, from_inner, c_send, c_recv, c, mate)

    def put(c, v):
        l = LD - M - 1 - c // PIECES
        v = v.astype(f32)
        start = c % PIECES * PIECE
        full = min(max(3 * CH - start, 0), PIECE)
        if full:
            grads[l, 0, start:start + full] = v[:full, :CH]
            grads[l, 1, start:start + full] = v[:full, CH:]
        if full < PIECE:
            low = start + full - 3 * CH
            grads[l, 2, low:low + PIECE - full] = v[full:, :CH]
            low = low + 3 * CH // 2
            grads[l, 2, low:low + PIECE - full] = v[full:, CH:]

    def pair_sum(c):
        part = (c // PIECES, pl.ds(c % PIECES * PIECE, PIECE))
        to_inner(c).wait_recv()
        half[part] = (own[part].astype(f32) + from_outer[part].astype(f32)).astype(bf16)
        to_across(c).start()

    def full_sum(c):
        part = (c // PIECES, pl.ds(c % PIECES * PIECE, PIECE))
        to_across(c).wait_recv()
        v = (half[part].astype(f32) + from_across[part].astype(f32)).astype(bf16)
        whole[part] = v
        to_outer(c).start()
        put(c, v)

    def replicated(q, i):
        l = LD - 1 - i
        pair = (2 * q, 2 * q + 1)
        if i == 0:
            e = jnp.concatenate([adjs[s] for s in pair], axis=1).astype(f32)
        else:
            e = rep[...]
        h = jnp.tanh(jnp.concatenate([far[s, i, n] for s in pair for n in range(samples)], axis=1).astype(f32))
        v = cols(e)
        if i < M - 1:
            rep[...] = e + STEP * (1.0 - h * h) * conv(weights[l], v)
        h = h.astype(bf16).astype(f32)
        h = jnp.concatenate([rows_down(h).astype(bf16), h.astype(bf16), rows_up(h).astype(bf16)], axis=0)
        return lax.dot_general(v, h, (((1,), (1,)), ((), ())), preferred_element_type=f32) * scale

    for i in range(LD):
        l = LD - 1 - i
        v = cols(p)
        p = p + slopes[l] * conv(weights[l], v)
        if i >= M:
            t = lax.dot_general(v, act_rows[l], (((1,), (1,)), ((), ())), preferred_element_type=f32) * scale
            own[i - M, :3 * CH] = t[:, :2 * CH].astype(bf16)
            own[i - M, 3 * CH:] = jnp.concatenate(
                [t[:3 * CH // 2, 2 * CH:], t[3 * CH // 2:, 2 * CH:]], axis=1).astype(bf16)

            @pl.when(outer)
            def _():
                for c in range((i - M) * PIECES, (i - M + 1) * PIECES):
                    to_inner(c).start()
    for n in range(samples):
        bottoms[0, n] = p[:, n * CELLS:(n + 1) * CELLS]

    adj_copy(mate, 0, mate).wait_recv()

    @pl.when(inner)
    def _():
        adj_forwards()[0].start()
        adj_copy(across, 0, mate).wait_recv()
        adj_forwards()[1].start()

    pass_on(len(forwards))
    for i in range(M):
        far_arrival(mate, i).wait_recv()

    lag = 2
    for u in range(2 * M):
        @pl.when(inner)
        def _():
            if u < chunks:
                pair_sum(u)
            if lag <= u < chunks + lag:
                full_sum(u - lag)
            if u == 1:
                adj_copy(3 - mate, 0, mate).wait_recv()
                adj_forwards()[2].start()

        if u == M:
            @pl.when(outer)
            def _():
                for s in (2 - 2 * near, 3 - 2 * near):
                    adj_copy(s, 0, mate).wait_recv()
                    for i in range(M):
                        far_arrival(s, i).wait_recv()

        l = LD - 1 - u % M
        t = replicated(near if u < M else 1 - near, u % M)
        for a in range(3):
            g = t[:, a * CH:(a + 1) * CH]
            grads[l, a] = g if u < M else grads[l, a] + g

    @pl.when(inner)
    def _():
        for u in range(2 * M, chunks + lag):
            if u < chunks:
                pair_sum(u)
            if u >= lag:
                full_sum(u - lag)
        for c in range(chunks):
            to_across(c).wait_send()
            to_outer(c).wait_send()
        adj_to_across().wait_send()
        for copy in adj_forwards():
            copy.wait_send()
        for n in (2, 3):
            for i in range(M):
                far_forward(i, n).wait_send()

    @pl.when(outer)
    def _():
        for c in range(chunks):
            to_outer(c).wait_recv()
            part = (c // PIECES, pl.ds(c % PIECES * PIECE, PIECE))
            put(c, from_inner[part])
        for c in range(chunks):
            to_inner(c).wait_send()

    adj_to_mate().wait_send()
    for i in range(M):
        for copy in far_sends(i):
            copy.wait_send()

    for lower in range(0, blocks - 2, 2):
        @pl.when(jnp.logical_and(base > lower, me < blocks - 1))
        def _():
            mean_copy(lower + core).wait_send()

    @pl.when(jnp.logical_and(core == 1, me < blocks - 1))
    def _():
        mean_copy(me - 1).wait_send()

    for j in range(2, blocks - 1):
        @pl.when(jnp.logical_and(base + 1 < j, core == j % 2))
        def _():
            forward(j).wait_send()

    for peer in range(blocks - 2):
        @pl.when(base > peer)
        def _():
            src_copy(peer, peer % 2).wait_send()

    @pl.when(core == 1)
    def _():
        src_copy(me - 1, 0).wait_send()

    @pl.when(jnp.logical_or(jnp.logical_not(last), core == 1))
    def _():
        swap.wait_send()


def write(corrected, bottoms, grads, corrected_out, bottoms_out, grads_out, sem):
    stores = [pltpu.make_async_copy(grads, grads_out, sem.at[0]),
              pltpu.make_async_copy(corrected, corrected_out, sem.at[1]),
              pltpu.make_async_copy(bottoms, bottoms_out, sem.at[2])]
    for store in stores:
        store.start()
    for store in stores:
        store.wait()


def body(blocks, parts, states, kernels, boundary):
    samples = states.shape[1]
    lanes = samples * CELLS
    chunks = (LD - M) * PIECES
    vmem = pl.BlockSpec(memory_space=pltpu.VMEM)
    hbm = pl.BlockSpec(memory_space=pltpu.HBM)
    dma = pltpu.SemaphoreType.DMA
    corrected, bottoms, grads = pl.pallas_call(
        functools.partial(kernel, blocks, parts, samples),
        out_shape=(
            jax.ShapeDtypeStruct(boundary.shape, f32),
            jax.ShapeDtypeStruct(boundary.shape, f32),
            jax.ShapeDtypeStruct((LD, 3, 3 * CH, CH), f32),
        ),
        in_specs=[hbm] * 3,
        out_specs=(vmem,) * 3,
        scratch_shapes=[
            pltpu.VMEM(states.shape, bf16),
            pltpu.VMEM((LD, 3, 3 * CH, CH), bf16),
            pltpu.VMEM(boundary.shape, f32),
            dma((3,)),
            pltpu.VMEM((LD, 3 * CH, 3 * CH), bf16),
            pltpu.VMEM((LD, CH, lanes), f32),
            pltpu.VMEM((LD, CH, lanes), bf16),
            pltpu.VMEM((LD - M, 3 * CH, lanes), bf16),
            pltpu.VMEM((9 * CH // 2, 2 * CH), bf16),
            pltpu.VMEM((blocks, 9 * CH // 2, 2 * CH), bf16),
            pltpu.VMEM((2, CH, lanes // 2), bf16),
            pltpu.VMEM((blocks, CH, lanes // 2), bf16),
            pltpu.VMEM((CH, lanes), f32),
            *[pltpu.VMEM((CH, lanes // 2), f32)] * 3,
            pltpu.VMEM((parts, M, samples, CH, CELLS), bf16),
            pltpu.VMEM((parts, CH, lanes), bf16),
            pltpu.VMEM((CH, 2 * lanes), f32),
            *[pltpu.VMEM((LD - M, PACKED, 2 * CH), bf16)] * 6,
            dma((4, M)), dma((parts, M)), dma((5,)), dma((parts,)),
            *[dma((blocks,))] * 5, dma, dma,
            *[dma((chunks,))] * 6,
        ],
        compiler_params=pltpu.CompilerParams(
            collective_id=0, has_side_effects=True, vmem_limit_bytes=40 * 1024 * 1024),
        cost_estimate=pl.CostEstimate(flops=2 * 10**9, bytes_accessed=6 * 10**6, transcendentals=262144),
        name="cycle",
    )(*[pltpu.with_memory_space_constraint(a, pltpu.HBM) for a in (states, kernels.reshape(LD, 3, 3 * CH, CH), boundary)])
    shapes = (corrected, bottoms, grads)
    corrected, bottoms, grads = pl.pallas_call(
        write,
        out_shape=tuple(jax.ShapeDtypeStruct(a.shape, a.dtype) for a in shapes),
        in_specs=[pl.BlockSpec(memory_space=pl.ANY)] * 3,
        out_specs=(hbm,) * 3,
        scratch_shapes=[dma((3,))],
        cost_estimate=pl.CostEstimate(flops=0, bytes_accessed=5 * 10**6, transcendentals=0),
        compiler_params=pltpu.CompilerParams(vmem_limit_bytes=4 * 1024 * 1024),
        name="write",
    )(*[pltpu.with_memory_space_constraint(a, pltpu.VMEM) for a in shapes])
    return corrected, bottoms, grads.reshape(LD, 9, CH, CH)


def solution(mesh):
    placed = (
        P("layer", "dp", None, None),
        P("layer", None, None, None),
        P("layer", "dp", None, None),
    )
    return jax.shard_map(
        functools.partial(body, mesh.shape["layer"], mesh.shape["dp"]),
        mesh=mesh,
        in_specs=placed,
        out_specs=(
            P("layer", "dp", None, None),
            P("layer", "dp", None, None),
            P("layer", None, None, None),
        ),
        check_vma=False,
    )
```

```python
import functools

import jax
import jax.numpy as jnp
from jax import lax
from jax.experimental import pallas as pl
from jax.experimental.pallas import tpu as pltpu
from jax.sharding import PartitionSpec as P

MAP = 16
CELLS = MAP * MAP
LD = 8
CH = 64
STEP = 0.5 / LD
MO = 3
MI = 3
PIECES = 2
LAG = 5
FWD = 3
EARLY = 1
PACKED = 9 * CH // 2
PIECE = PACKED // PIECES
MESH_ID = pl.DeviceIdType.MESH
f32, bf16 = jnp.float32, jnp.bfloat16


def kernel(blocks, parts, samples, states_in, kernels_in, boundary_in, corrected, bottoms, grads,
           states, kernels, boundary, in_sem, mean_w, weights, slopes, acts, act_rows, mean_own, means, src_own, srcs,
           adj, chain, swap_out, swap_in, far, adjs, rep, own, from_outer, half, from_across, whole, from_inner,
           far_send, far_recv, adj_send, adj_recv, mean_send, mean_recv, fwd_send, src_send, src_recv, swap_send, swap_recv,
           a_send, a_recv, b_send, b_recv, c_send, c_recv):
    me = lax.axis_index("layer")
    dp = lax.axis_index("dp")
    lanes = samples * CELLS
    width = lanes // 2
    core = lax.rem(me, 2)
    base = me - core
    other = me + 1 - 2 * core
    last = base == blocks - 2
    inner = jnp.logical_or(dp == 1, dp == 2)
    outer = jnp.logical_or(dp == 0, dp == 3)
    mate = dp + 1 - 2 * lax.rem(dp, 2)
    across = 3 - dp
    near = lax.div(dp, 2)

    barrier = pltpu.get_barrier_semaphore()
    for i in range(1, blocks):
        pl.semaphore_signal(barrier, inc=1, device_id=(lax.rem(me + i, blocks), dp), device_id_type=MESH_ID)
    for i in range(1, parts):
        pl.semaphore_signal(barrier, inc=1, device_id=(me, lax.rem(dp + i, parts)), device_id_type=MESH_ID)

    loads = [pltpu.make_async_copy(kernels_in, kernels, in_sem.at[0]),
             pltpu.make_async_copy(boundary_in, boundary, in_sem.at[1]),
             pltpu.make_async_copy(states_in, states, in_sem.at[2])]
    for load in loads:
        load.start()

    cell = lax.broadcasted_iota(jnp.int32, (CH, CELLS), 1)
    col = lax.bitwise_and(cell[:, :2 * CH], MAP - 1)
    row = lax.shift_right_logical(cell, 4)
    col_lo, col_hi = col >= 1, col <= MAP - 2
    row_lo, row_hi = row >= 1, row <= MAP - 2

    def cols(v):
        pieces = [v[:, k:k + 2 * CH] for k in range(0, v.shape[1], 2 * CH)]
        left = [jnp.where(col_hi, pltpu.roll(x, 2 * CH - 1, 1), 0.0).astype(bf16) for x in pieces]
        right = [jnp.where(col_lo, pltpu.roll(x, 1, 1), 0.0).astype(bf16) for x in pieces]
        return jnp.concatenate(
            [jnp.concatenate(left, axis=1), v.astype(bf16), jnp.concatenate(right, axis=1)], axis=0)

    def by_sample(f, v):
        return jnp.concatenate([f(v[:, k:k + CELLS]) for k in range(0, v.shape[1], CELLS)], axis=1)

    def rows_up(v):
        return by_sample(lambda x: jnp.where(row_hi, pltpu.roll(x, CELLS - MAP, 1), 0.0), v)

    def rows_down(v):
        return by_sample(lambda x: jnp.where(row_lo, pltpu.roll(x, MAP, 1), 0.0), v)

    def conv(w, v):
        r = jnp.dot(w, v, preferred_element_type=f32)
        return rows_up(r[:CH]) + r[CH:2 * CH] + rows_down(r[2 * CH:])

    def step(ps, vs, l):
        return [q + slopes[l, :, n * CELLS:(n + 1) * CELLS] * conv(weights[l], v)
                for n, (q, v) in enumerate(zip(ps, vs))]

    def flat(ref):
        return jnp.concatenate([ref[n] for n in range(samples)], axis=1)

    def turned(ks):
        return jnp.concatenate([k.astype(bf16) for k in ks], axis=1).T

    loads[0].wait()
    total = [kernels[0, a].astype(f32) for a in range(3)]
    for l in range(1, LD):
        for a in range(3):
            total[a] = total[a] + kernels[l, a].astype(f32)
    mean = turned([t * (1.0 / LD) for t in total])
    mean_own[:3 * CH] = mean[:, :2 * CH]
    mean_own[3 * CH:] = jnp.concatenate([mean[:3 * CH // 2, 2 * CH:], mean[3 * CH // 2:, 2 * CH:]], axis=1)

    def unpacked(m):
        tail = jnp.concatenate([m[3 * CH:, :CH], m[3 * CH:, CH:]], axis=0)
        return jnp.concatenate([m[:3 * CH], tail], axis=1)

    def first(ps, l):
        weights[l] = turned([kernels[l, a] for a in range(3)])
        h = jnp.tanh(flat(states.at[l]).astype(f32))
        slope = STEP * (1.0 - h * h)
        acts[l] = h.astype(bf16)
        slopes[l] = slope
        return step(ps, [cols(q) for q in ps], l)

    loads[1].wait()
    loads[2].wait()
    top = flat(boundary.at[0])
    ps = [boundary[0, n] for n in range(samples)]
    for l in reversed(range(LD - EARLY, LD)):
        ps = first(ps, l)

    pl.semaphore_wait(barrier, blocks - 1 + parts - 1)

    def mean_copy(peer):
        return pltpu.make_async_remote_copy(
            src_ref=mean_own, dst_ref=means.at[me], send_sem=mean_send.at[peer],
            recv_sem=mean_recv.at[me], device_id=(peer, dp), device_id_type=MESH_ID)

    def src_copy(peer, part):
        return pltpu.make_async_remote_copy(
            src_ref=src_own.at[part], dst_ref=srcs.at[me], send_sem=src_send.at[peer],
            recv_sem=src_recv.at[me], device_id=(peer, dp), device_id_type=MESH_ID)

    def mean_arrival(j):
        return pltpu.make_async_remote_copy(
            src_ref=mean_own, dst_ref=means.at[j], send_sem=mean_send.at[0],
            recv_sem=mean_recv.at[j], device_id=(other, dp), device_id_type=MESH_ID)

    def src_arrival(j):
        return pltpu.make_async_remote_copy(
            src_ref=src_own.at[0], dst_ref=srcs.at[j], send_sem=src_send.at[0],
            recv_sem=src_recv.at[j], device_id=(other, dp), device_id_type=MESH_ID)

    def far_copy(src, s, i, n, peer):
        return pltpu.make_async_remote_copy(
            src_ref=src, dst_ref=far.at[s, i], send_sem=far_send.at[n, i], recv_sem=far_recv.at[s, i],
            device_id=(me, peer), device_id_type=MESH_ID)

    def far_sends(i):
        src = states.at[LD - 1 - i]
        return far_copy(src, dp, i, 0, 2 - near), far_copy(src, dp, i, 1, mate)

    def far_forward(i, n):
        s = across if n == 2 else 3 - mate
        return far_copy(far.at[s, i], s, i, n, mate)

    def far_arrival(s, i):
        return far_copy(far.at[s, i], s, i, 0, mate)

    def adj_copy(s, n, peer):
        return pltpu.make_async_remote_copy(
            src_ref=adjs.at[s], dst_ref=adjs.at[s], send_sem=adj_send.at[n], recv_sem=adj_recv.at[s],
            device_id=(me, peer), device_id_type=MESH_ID)

    def adj_to_mate():
        return adj_copy(dp, 0, mate)

    def adj_to_across():
        return adj_copy(dp, 1, across)

    def adj_forwards():
        return adj_copy(mate, 2, across), adj_copy(across, 3, mate), adj_copy(3 - mate, 4, mate)

    forwards = [(i, n) for i in range(MO) for n in (2, 3)]

    def pass_on(count):
        for i, n in forwards[:count]:
            @pl.when(inner)
            def _():
                far_arrival(across if n == 2 else 3 - mate, i).wait_recv()
                far_forward(i, n).start()
        del forwards[:count]

    swap = pltpu.make_async_remote_copy(
        src_ref=swap_out, dst_ref=swap_in, send_sem=swap_send, recv_sem=swap_recv,
        device_id=(other, dp), device_id_type=MESH_ID)

    def forward(j):
        return pltpu.make_async_remote_copy(
            src_ref=means.at[j], dst_ref=means.at[j], send_sem=fwd_send.at[j],
            recv_sem=mean_recv.at[j], device_id=(other, dp), device_id_type=MESH_ID)

    for lower in range(0, blocks - 2, 2):
        @pl.when(jnp.logical_and(base > lower, me < blocks - 1))
        def _():
            mean_copy(lower + core).start()

    @pl.when(jnp.logical_and(core == 1, me < blocks - 1))
    def _():
        mean_copy(me - 1).start()

    for i in range(MI):
        to_near, to_mate = far_sends(i)
        to_near.start()
        if i < MO:
            to_mate.start()
        else:
            @pl.when(outer)
            def _():
                to_mate.start()
        far[dp, i] = states[LD - 1 - i]

    for l in reversed(range(LD - EARLY)):
        ps = first(ps, l)
    p = jnp.concatenate(ps, axis=1)
    mean_w[me] = mean
    coarse = top + 0.5 * conv(mean, cols(top))
    source = p - jnp.where(me == blocks - 1, 0.0, coarse)
    for part in range(2):
        src_own[part] = source[:, part * width:(part + 1) * width].astype(bf16)

    @pl.when(core == 1)
    def _():
        src_copy(me - 1, 0).start()

    for peer in range(blocks - 2):
        @pl.when(base > peer)
        def _():
            src_copy(peer, peer % 2).start()

    @pl.when(jnp.logical_and(last, core == 1))
    def _():
        swap_out[...] = source[:, width:]
        swap.start()

    for j in reversed(range(2, blocks - 1)):
        @pl.when(jnp.logical_and(base + 1 < j, core == j % 2))
        def _():
            mean_arrival(j).wait_recv()
            forward(j).start()
            mean_w[j] = unpacked(means[j])

    pass_on(1)
    for l in range(LD - MI):
        h = acts[l].astype(f32)
        act_rows[l] = jnp.concatenate(
            [rows_down(h).astype(bf16), h.astype(bf16), rows_up(h).astype(bf16)], axis=0)

    for j in reversed(range(2, blocks - 1)):
        @pl.when(jnp.logical_and(base + 1 < j, core != j % 2))
        def _():
            mean_arrival(j).wait_recv()
            mean_w[j] = unpacked(means[j])

    @pl.when(jnp.logical_and(jnp.logical_not(last), core == 0))
    def _():
        mean_arrival(me + 1).wait_recv()
        mean_w[me + 1] = unpacked(means[me + 1])

    @pl.when(last)
    def _():
        @pl.when(core == 1)
        def _():
            adj[...] = top

        @pl.when(core == 0)
        def _():
            src_arrival(blocks - 1).wait_recv()
            adj[:, :width] = srcs[blocks - 1].astype(f32)
            swap.wait_recv()
            adj[:, width:] = swap_in[...]

    @pl.when(jnp.logical_not(last))
    def _():
        src_arrival(blocks - 1).wait_recv()
        chain[...] = srcs[blocks - 1].astype(f32)

    for j in reversed(range(2, blocks - 1)):
        pass_on(1 if 0 < blocks - 2 - j < 5 else 0)

        @pl.when(base + 1 < j)
        def _():
            e = chain[...]
            e = e + 0.5 * conv(mean_w[j], cols(e))
            src_arrival(j).wait_recv()
            chain[...] = e + srcs[j].astype(f32)

    @pl.when(jnp.logical_and(jnp.logical_not(last), core == 0))
    def _():
        e = chain[...]
        swap_out[...] = e
        swap.start()
        src_arrival(me + 1).wait_recv()
        adj[:, :width] = e + 0.5 * conv(mean_w[me + 1], cols(e)) + srcs[me + 1].astype(f32)
        swap.wait_recv()
        adj[:, width:] = swap_in[...]

    @pl.when(jnp.logical_and(jnp.logical_not(last), core == 1))
    def _():
        e = chain[...]
        swap_out[...] = e + 0.5 * conv(mean_w[me], cols(e)) + src_own[1].astype(f32)
        swap.start()
        adj[:, width:] = e
        swap.wait_recv()
        adj[:, :width] = swap_in[...]

    p = adj[...]
    adjs[dp] = p.astype(bf16)
    adj_to_mate().start()

    @pl.when(inner)
    def _():
        adj_to_across().start()

    for n in range(samples):
        corrected[0, n] = p[:, n * CELLS:(n + 1) * CELLS]

    scale = STEP / (samples * parts)
    chunks = (LD - MO) * PIECES
    summed = (MI - MO) * PIECES

    def hop(src, dst, send, recv, c, peer):
        part = (c // PIECES, pl.ds(c % PIECES * PIECE, PIECE))
        return pltpu.make_async_remote_copy(
            src_ref=src.at[part], dst_ref=dst.at[part], send_sem=send.at[c], recv_sem=recv.at[c],
            device_id=(me, peer), device_id_type=MESH_ID)

    def to_inner(c):
        return hop(own, from_outer, a_send, a_recv, c, mate)

    def to_across(c):
        return hop(half, from_across, b_send, b_recv, c, across)

    def to_outer(c):
        return hop(whole, from_inner, c_send, c_recv, c, mate)

    def put(c, v):
        l = LD - MO - 1 - c // PIECES
        v = v.astype(f32)
        start = c % PIECES * PIECE
        full = min(max(3 * CH - start, 0), PIECE)
        if full:
            grads[l, 0, start:start + full] = v[:full, :CH]
            grads[l, 1, start:start + full] = v[:full, CH:]
        if full < PIECE:
            low = start + full - 3 * CH
            grads[l, 2, low:low + PIECE - full] = v[full:, :CH]
            low = low + 3 * CH // 2
            grads[l, 2, low:low + PIECE - full] = v[full:, CH:]

    def pair_sum(c):
        part = (c // PIECES, pl.ds(c % PIECES * PIECE, PIECE))
        to_inner(c).wait_recv()
        half[part] = (own[part].astype(f32) + from_outer[part].astype(f32)).astype(bf16)
        to_across(c).start()

    def full_sum(c):
        part = (c // PIECES, pl.ds(c % PIECES * PIECE, PIECE))
        to_across(c).wait_recv()
        v = (half[part].astype(f32) + from_across[part].astype(f32)).astype(bf16)
        whole[part] = v
        to_outer(c).start()
        put(c, v)

    def replicated(q, i):
        l = LD - 1 - i
        pair = (2 * q, 2 * q + 1)
        if i == 0:
            e = jnp.concatenate([adjs[s] for s in pair], axis=1).astype(f32)
        else:
            e = rep[...]
        h = jnp.tanh(jnp.concatenate([far[s, i, n] for s in pair for n in range(samples)], axis=1).astype(f32))
        v = cols(e)
        if i < MI - 1:
            rep[...] = e + STEP * (1.0 - h * h) * conv(weights[l], v)
        h = h.astype(bf16).astype(f32)
        h = jnp.concatenate([rows_down(h).astype(bf16), h.astype(bf16), rows_up(h).astype(bf16)], axis=0)
        return lax.dot_general(v, h, (((1,), (1,)), ((), ())), preferred_element_type=f32) * scale

    def packed(t):
        low = jnp.concatenate([t[:3 * CH // 2, 2 * CH:], t[3 * CH // 2:, 2 * CH:]], axis=1)
        return jnp.concatenate([t[:, :2 * CH], low], axis=0).astype(bf16)

    ps = [p[:, n * CELLS:(n + 1) * CELLS] for n in range(samples)]
    for i in range(LD):
        l = LD - 1 - i
        vs = [cols(q) for q in ps]
        ps = step(ps, vs, l)
        if i >= MI:
            v = jnp.concatenate(vs, axis=1)
            t = lax.dot_general(v, act_rows[l], (((1,), (1,)), ((), ())), preferred_element_type=f32) * scale
            own[i - MO] = packed(t)

            @pl.when(outer)
            def _():
                for c in range((i - MO) * PIECES, (i - MO + 1) * PIECES):
                    to_inner(c).start()
    for n in range(samples):
        bottoms[0, n] = ps[n]

    adj_copy(mate, 0, mate).wait_recv()

    @pl.when(inner)
    def _():
        adj_forwards()[0].start()
        adj_copy(across, 0, mate).wait_recv()
        adj_forwards()[1].start()

    pass_on(len(forwards))
    for i in range(MO):
        far_arrival(mate, i).wait_recv()

    @pl.when(inner)
    def _():
        for i in range(MO, MI):
            for j in range(1, parts):
                far_arrival(lax.rem(dp + j, parts), i).wait_recv()

    def sums(u):
        if summed + u < chunks:
            pair_sum(summed + u)
        if u >= LAG and summed + u - LAG < chunks:
            full_sum(summed + u - LAG)

    def accumulate(half_, i):
        l = LD - 1 - i
        t = replicated(near if half_ == 0 else 1 - near, i)
        gs = [t[:, a * CH:(a + 1) * CH] for a in range(3)]
        if half_ == 1:
            gs = [grads[l, a] + gs[a] for a in range(3)]
        if half_ == 1 and i >= MO:
            g = i - MO
            v = packed(jnp.concatenate(gs, axis=1))
            whole[g] = v
            for c in range(g * PIECES, (g + 1) * PIECES):
                to_outer(c).start()
                start = c % PIECES * PIECE
                put(c, v[start:start + PIECE])
        else:
            for a in range(3):
                grads[l, a] = gs[a]

    def units(half_):
        for i in range(MO):
            accumulate(half_, i)
        if MI > MO:
            @pl.when(inner)
            def _():
                for i in range(MO, MI):
                    accumulate(half_, i)

    units(0)

    @pl.when(inner)
    def _():
        for u in range(chunks - summed + LAG):
            sums(u)
            if u == FWD:
                adj_copy(3 - mate, 0, mate).wait_recv()
                adj_forwards()[2].start()

    @pl.when(outer)
    def _():
        for s in (2 - 2 * near, 3 - 2 * near):
            adj_copy(s, 0, mate).wait_recv()
            for i in range(MO):
                far_arrival(s, i).wait_recv()

    units(1)

    @pl.when(inner)
    def _():
        for c in range(chunks):
            if c >= summed:
                to_across(c).wait_send()
            to_outer(c).wait_send()
        adj_to_across().wait_send()
        for copy in adj_forwards():
            copy.wait_send()
        for n in (2, 3):
            for i in range(MO):
                far_forward(i, n).wait_send()

    @pl.when(outer)
    def _():
        for c in range(chunks):
            to_outer(c).wait_recv()
            part = (c // PIECES, pl.ds(c % PIECES * PIECE, PIECE))
            put(c, from_inner[part])
        for c in range(summed, chunks):
            to_inner(c).wait_send()

    adj_to_mate().wait_send()
    for i in range(MI):
        to_near, to_mate = far_sends(i)
        to_near.wait_send()
        if i < MO:
            to_mate.wait_send()
        else:
            @pl.when(outer)
            def _():
                to_mate.wait_send()

    for lower in range(0, blocks - 2, 2):
        @pl.when(jnp.logical_and(base > lower, me < blocks - 1))
        def _():
            mean_copy(lower + core).wait_send()

    @pl.when(jnp.logical_and(core == 1, me < blocks - 1))
    def _():
        mean_copy(me - 1).wait_send()

    for j in range(2, blocks - 1):
        @pl.when(jnp.logical_and(base + 1 < j, core == j % 2))
        def _():
            forward(j).wait_send()

    for peer in range(blocks - 2):
        @pl.when(base > peer)
        def _():
            src_copy(peer, peer % 2).wait_send()

    @pl.when(core == 1)
    def _():
        src_copy(me - 1, 0).wait_send()

    @pl.when(jnp.logical_or(jnp.logical_not(last), core == 1))
    def _():
        swap.wait_send()


def write(corrected, bottoms, grads, corrected_out, bottoms_out, grads_out, sem):
    stores = [pltpu.make_async_copy(grads, grads_out, sem.at[0]),
              pltpu.make_async_copy(corrected, corrected_out, sem.at[1]),
              pltpu.make_async_copy(bottoms, bottoms_out, sem.at[2])]
    for store in stores:
        store.start()
    for store in stores:
        store.wait()


def body(blocks, parts, states, kernels, boundary):
    samples = states.shape[1]
    lanes = samples * CELLS
    chunks = (LD - MO) * PIECES
    vmem = pl.BlockSpec(memory_space=pltpu.VMEM)
    hbm = pl.BlockSpec(memory_space=pltpu.HBM)
    dma = pltpu.SemaphoreType.DMA
    corrected, bottoms, grads = pl.pallas_call(
        functools.partial(kernel, blocks, parts, samples),
        out_shape=(
            jax.ShapeDtypeStruct(boundary.shape, f32),
            jax.ShapeDtypeStruct(boundary.shape, f32),
            jax.ShapeDtypeStruct((LD, 3, 3 * CH, CH), f32),
        ),
        in_specs=[hbm] * 3,
        out_specs=(vmem,) * 3,
        scratch_shapes=[
            pltpu.VMEM(states.shape, bf16),
            pltpu.VMEM((LD, 3, 3 * CH, CH), bf16),
            pltpu.VMEM(boundary.shape, f32),
            dma((3,)),
            pltpu.VMEM((blocks, 3 * CH, 3 * CH), bf16),
            pltpu.VMEM((LD, 3 * CH, 3 * CH), bf16),
            pltpu.VMEM((LD, CH, lanes), f32),
            pltpu.VMEM((LD, CH, lanes), bf16),
            pltpu.VMEM((LD - MI, 3 * CH, lanes), bf16),
            pltpu.VMEM((9 * CH // 2, 2 * CH), bf16),
            pltpu.VMEM((blocks, 9 * CH // 2, 2 * CH), bf16),
            pltpu.VMEM((2, CH, lanes // 2), bf16),
            pltpu.VMEM((blocks, CH, lanes // 2), bf16),
            pltpu.VMEM((CH, lanes), f32),
            *[pltpu.VMEM((CH, lanes // 2), f32)] * 3,
            pltpu.VMEM((parts, MI, samples, CH, CELLS), bf16),
            pltpu.VMEM((parts, CH, lanes), bf16),
            pltpu.VMEM((CH, 2 * lanes), f32),
            *[pltpu.VMEM((LD - MO, PACKED, 2 * CH), bf16)] * 6,
            dma((4, MI)), dma((parts, MI)), dma((5,)), dma((parts,)),
            *[dma((blocks,))] * 5, dma, dma,
            *[dma((chunks,))] * 6,
        ],
        compiler_params=pltpu.CompilerParams(
            collective_id=0, has_side_effects=True, vmem_limit_bytes=40 * 1024 * 1024),
        cost_estimate=pl.CostEstimate(flops=2 * 10**9, bytes_accessed=6 * 10**6, transcendentals=262144),
        name="cycle",
    )(*[pltpu.with_memory_space_constraint(a, pltpu.HBM) for a in (states, kernels.reshape(LD, 3, 3 * CH, CH), boundary)])
    shapes = (corrected, bottoms, grads)
    corrected, bottoms, grads = pl.pallas_call(
        write,
        out_shape=tuple(jax.ShapeDtypeStruct(a.shape, a.dtype) for a in shapes),
        in_specs=[pl.BlockSpec(memory_space=pl.ANY)] * 3,
        out_specs=(hbm,) * 3,
        scratch_shapes=[dma((3,))],
        cost_estimate=pl.CostEstimate(flops=0, bytes_accessed=5 * 10**6, transcendentals=0),
        compiler_params=pltpu.CompilerParams(vmem_limit_bytes=4 * 1024 * 1024),
        name="write",
    )(*[pltpu.with_memory_space_constraint(a, pltpu.VMEM) for a in shapes])
    return corrected, bottoms, grads.reshape(LD, 9, CH, CH)


def solution(mesh):
    placed = (
        P("layer", "dp", None, None),
        P("layer", None, None, None),
        P("layer", "dp", None, None),
    )
    return jax.shard_map(
        functools.partial(body, mesh.shape["layer"], mesh.shape["dp"]),
        mesh=mesh,
        in_specs=placed,
        out_specs=(
            P("layer", "dp", None, None),
            P("layer", "dp", None, None),
            P("layer", None, None, None),
        ),
        check_vma=False,
    )
```

```python
import functools

import jax
import jax.numpy as jnp
from jax import lax
from jax.experimental import pallas as pl
from jax.experimental.pallas import tpu as pltpu
from jax.sharding import PartitionSpec as P

MAP = 16
CELLS = MAP * MAP
LD = 8
CH = 64
STEP = 0.5 / LD
MO = 3
MI = 3
PIECES = 2
LAG = 5
FWD = 3
EARLY = 1
PACKED = 9 * CH // 2
PIECE = PACKED // PIECES
MESH_ID = pl.DeviceIdType.MESH
f32, bf16 = jnp.float32, jnp.bfloat16


def kernel(blocks, parts, samples, states_in, kernels_in, boundary_in, corrected, bottoms, grads,
           states, kernels, boundary, in_sem, mean_w, weights, slopes, acts, act_rows, mean_own, means, src_own, srcs,
           adj, chain, swap_out, swap_in, far, adjs, rep, own, from_outer, half, from_across, whole, from_inner,
           far_send, far_recv, adj_send, adj_recv, mean_send, mean_recv, fwd_send, src_send, src_recv, swap_send, swap_recv,
           a_send, a_recv, b_send, b_recv, c_send, c_recv):
    me = lax.axis_index("layer")
    dp = lax.axis_index("dp")
    lanes = samples * CELLS
    width = lanes // 2
    core = lax.rem(me, 2)
    base = me - core
    other = me + 1 - 2 * core
    last = base == blocks - 2
    inner = jnp.logical_or(dp == 1, dp == 2)
    outer = jnp.logical_or(dp == 0, dp == 3)
    mate = dp + 1 - 2 * lax.rem(dp, 2)
    across = 3 - dp
    near = lax.div(dp, 2)

    barrier = pltpu.get_barrier_semaphore()
    for i in range(1, blocks):
        pl.semaphore_signal(barrier, inc=1, device_id=(lax.rem(me + i, blocks), dp), device_id_type=MESH_ID)
    for i in range(1, parts):
        pl.semaphore_signal(barrier, inc=1, device_id=(me, lax.rem(dp + i, parts)), device_id_type=MESH_ID)

    loads = [pltpu.make_async_copy(kernels_in, kernels, in_sem.at[0]),
             pltpu.make_async_copy(boundary_in, boundary, in_sem.at[1]),
             pltpu.make_async_copy(states_in, states, in_sem.at[2])]
    for load in loads:
        load.start()

    cell = lax.broadcasted_iota(jnp.int32, (CH, CELLS), 1)
    col = lax.bitwise_and(cell[:, :2 * CH], MAP - 1)
    row = lax.shift_right_logical(cell, 4)
    col_lo, col_hi = col >= 1, col <= MAP - 2
    row_lo, row_hi = row >= 1, row <= MAP - 2

    def cols(v):
        pieces = [v[:, k:k + 2 * CH] for k in range(0, v.shape[1], 2 * CH)]
        left = [jnp.where(col_hi, pltpu.roll(x, 2 * CH - 1, 1), 0.0).astype(bf16) for x in pieces]
        right = [jnp.where(col_lo, pltpu.roll(x, 1, 1), 0.0).astype(bf16) for x in pieces]
        return jnp.concatenate(
            [jnp.concatenate(left, axis=1), v.astype(bf16), jnp.concatenate(right, axis=1)], axis=0)

    def by_sample(f, v):
        return jnp.concatenate([f(v[:, k:k + CELLS]) for k in range(0, v.shape[1], CELLS)], axis=1)

    def rows_up(v):
        return by_sample(lambda x: jnp.where(row_hi, pltpu.roll(x, CELLS - MAP, 1), 0.0), v)

    def rows_down(v):
        return by_sample(lambda x: jnp.where(row_lo, pltpu.roll(x, MAP, 1), 0.0), v)

    def conv(w, v):
        r = jnp.dot(w, v, preferred_element_type=f32)
        return rows_up(r[:CH]) + r[CH:2 * CH] + rows_down(r[2 * CH:])

    def step(ps, vs, l):
        return [q + slopes[l, :, n * CELLS:(n + 1) * CELLS] * conv(weights[l], v)
                for n, (q, v) in enumerate(zip(ps, vs))]

    def flat(ref):
        return jnp.concatenate([ref[n] for n in range(samples)], axis=1)

    def turned(ks):
        return jnp.concatenate([k.astype(bf16) for k in ks], axis=1).T

    loads[0].wait()
    total = [kernels[0, a].astype(f32) for a in range(3)]
    for l in range(1, LD):
        for a in range(3):
            total[a] = total[a] + kernels[l, a].astype(f32)
    mean = turned([t * (1.0 / LD) for t in total])
    mean_own[:3 * CH] = mean[:, :2 * CH]
    mean_own[3 * CH:] = jnp.concatenate([mean[:3 * CH // 2, 2 * CH:], mean[3 * CH // 2:, 2 * CH:]], axis=1)

    def unpacked(m):
        tail = jnp.concatenate([m[3 * CH:, :CH], m[3 * CH:, CH:]], axis=0)
        return jnp.concatenate([m[:3 * CH], tail], axis=1)

    def first(ps, l):
        weights[l] = turned([kernels[l, a] for a in range(3)])
        h = jnp.tanh(flat(states.at[l]).astype(f32))
        slope = STEP * (1.0 - h * h)
        acts[l] = h.astype(bf16)
        slopes[l] = slope
        return step(ps, [cols(q) for q in ps], l)

    loads[1].wait()
    loads[2].wait()
    top = flat(boundary.at[0])
    ps = [boundary[0, n] for n in range(samples)]
    for l in reversed(range(LD - EARLY, LD)):
        ps = first(ps, l)

    pl.semaphore_wait(barrier, blocks - 1 + parts - 1)

    def mean_copy(peer):
        return pltpu.make_async_remote_copy(
            src_ref=mean_own, dst_ref=means.at[me], send_sem=mean_send.at[peer],
            recv_sem=mean_recv.at[me], device_id=(peer, dp), device_id_type=MESH_ID)

    def src_copy(peer, part):
        return pltpu.make_async_remote_copy(
            src_ref=src_own.at[part], dst_ref=srcs.at[me], send_sem=src_send.at[peer],
            recv_sem=src_recv.at[me], device_id=(peer, dp), device_id_type=MESH_ID)

    def mean_arrival(j):
        return pltpu.make_async_remote_copy(
            src_ref=mean_own, dst_ref=means.at[j], send_sem=mean_send.at[0],
            recv_sem=mean_recv.at[j], device_id=(other, dp), device_id_type=MESH_ID)

    def src_arrival(j):
        return pltpu.make_async_remote_copy(
            src_ref=src_own.at[0], dst_ref=srcs.at[j], send_sem=src_send.at[0],
            recv_sem=src_recv.at[j], device_id=(other, dp), device_id_type=MESH_ID)

    def far_copy(src, s, i, n, peer):
        return pltpu.make_async_remote_copy(
            src_ref=src, dst_ref=far.at[s, i], send_sem=far_send.at[n, i], recv_sem=far_recv.at[s, i],
            device_id=(me, peer), device_id_type=MESH_ID)

    def far_sends(i):
        src = states.at[LD - 1 - i]
        return far_copy(src, dp, i, 0, 2 - near), far_copy(src, dp, i, 1, mate)

    def far_forward(i, n):
        s = across if n == 2 else 3 - mate
        return far_copy(far.at[s, i], s, i, n, mate)

    def far_arrival(s, i):
        return far_copy(far.at[s, i], s, i, 0, mate)

    def adj_copy(s, n, peer):
        return pltpu.make_async_remote_copy(
            src_ref=adjs.at[s], dst_ref=adjs.at[s], send_sem=adj_send.at[n], recv_sem=adj_recv.at[s],
            device_id=(me, peer), device_id_type=MESH_ID)

    def adj_to_mate():
        return adj_copy(dp, 0, mate)

    def adj_to_across():
        return adj_copy(dp, 1, across)

    def adj_forwards():
        return adj_copy(mate, 2, across), adj_copy(across, 3, mate), adj_copy(3 - mate, 4, mate)

    forwards = [(i, n) for i in range(MO) for n in (2, 3)]

    def pass_on(count):
        for i, n in forwards[:count]:
            @pl.when(inner)
            def _():
                far_arrival(across if n == 2 else 3 - mate, i).wait_recv()
                far_forward(i, n).start()
        del forwards[:count]

    swap = pltpu.make_async_remote_copy(
        src_ref=swap_out, dst_ref=swap_in, send_sem=swap_send, recv_sem=swap_recv,
        device_id=(other, dp), device_id_type=MESH_ID)

    def forward(j):
        return pltpu.make_async_remote_copy(
            src_ref=means.at[j], dst_ref=means.at[j], send_sem=fwd_send.at[j],
            recv_sem=mean_recv.at[j], device_id=(other, dp), device_id_type=MESH_ID)

    for lower in range(0, blocks - 2, 2):
        @pl.when(jnp.logical_and(base > lower, me < blocks - 1))
        def _():
            mean_copy(lower + core).start()

    @pl.when(jnp.logical_and(core == 1, me < blocks - 1))
    def _():
        mean_copy(me - 1).start()

    for i in range(MI):
        to_near, to_mate = far_sends(i)
        to_mate.start()
        to_near.start()
        far[dp, i] = states[LD - 1 - i]

    for l in reversed(range(LD - EARLY)):
        ps = first(ps, l)
    p = jnp.concatenate(ps, axis=1)
    mean_w[me] = mean
    coarse = top + 0.5 * conv(mean, cols(top))
    source = p - jnp.where(me == blocks - 1, 0.0, coarse)
    for part in range(2):
        src_own[part] = source[:, part * width:(part + 1) * width].astype(bf16)

    @pl.when(core == 1)
    def _():
        src_copy(me - 1, 0).start()

    for peer in range(blocks - 2):
        @pl.when(base > peer)
        def _():
            src_copy(peer, peer % 2).start()

    @pl.when(jnp.logical_and(last, core == 1))
    def _():
        swap_out[...] = source[:, width:]
        swap.start()

    for j in reversed(range(2, blocks - 1)):
        @pl.when(jnp.logical_and(base + 1 < j, core == j % 2))
        def _():
            mean_arrival(j).wait_recv()
            forward(j).start()
            mean_w[j] = unpacked(means[j])

    pass_on(1)
    for l in range(LD - MI):
        h = acts[l].astype(f32)
        act_rows[l] = jnp.concatenate(
            [rows_down(h).astype(bf16), h.astype(bf16), rows_up(h).astype(bf16)], axis=0)

    for j in reversed(range(2, blocks - 1)):
        @pl.when(jnp.logical_and(base + 1 < j, core != j % 2))
        def _():
            mean_arrival(j).wait_recv()
            mean_w[j] = unpacked(means[j])

    @pl.when(jnp.logical_and(jnp.logical_not(last), core == 0))
    def _():
        mean_arrival(me + 1).wait_recv()
        mean_w[me + 1] = unpacked(means[me + 1])

    @pl.when(last)
    def _():
        @pl.when(core == 1)
        def _():
            adj[...] = top

        @pl.when(core == 0)
        def _():
            src_arrival(blocks - 1).wait_recv()
            adj[:, :width] = srcs[blocks - 1].astype(f32)
            swap.wait_recv()
            adj[:, width:] = swap_in[...]

    @pl.when(jnp.logical_not(last))
    def _():
        src_arrival(blocks - 1).wait_recv()
        chain[...] = srcs[blocks - 1].astype(f32)

    for j in reversed(range(2, blocks - 1)):
        pass_on(1 if 0 < blocks - 2 - j < 5 else 0)

        @pl.when(base + 1 < j)
        def _():
            e = chain[...]
            e = e + 0.5 * conv(mean_w[j], cols(e))
            src_arrival(j).wait_recv()
            chain[...] = e + srcs[j].astype(f32)

    @pl.when(jnp.logical_and(jnp.logical_not(last), core == 0))
    def _():
        e = chain[...]
        swap_out[...] = e
        swap.start()
        src_arrival(me + 1).wait_recv()
        adj[:, :width] = e + 0.5 * conv(mean_w[me + 1], cols(e)) + srcs[me + 1].astype(f32)
        swap.wait_recv()
        adj[:, width:] = swap_in[...]

    @pl.when(jnp.logical_and(jnp.logical_not(last), core == 1))
    def _():
        e = chain[...]
        swap_out[...] = e + 0.5 * conv(mean_w[me], cols(e)) + src_own[1].astype(f32)
        swap.start()
        adj[:, width:] = e
        swap.wait_recv()
        adj[:, :width] = swap_in[...]

    p = adj[...]
    adjs[dp] = p.astype(bf16)
    adj_to_mate().start()

    @pl.when(inner)
    def _():
        adj_to_across().start()

    for n in range(samples):
        corrected[0, n] = p[:, n * CELLS:(n + 1) * CELLS]

    scale = STEP / (samples * parts)
    chunks = (LD - MO) * PIECES
    summed = (MI - MO) * PIECES

    def hop(src, dst, send, recv, c, peer):
        part = (c // PIECES, pl.ds(c % PIECES * PIECE, PIECE))
        return pltpu.make_async_remote_copy(
            src_ref=src.at[part], dst_ref=dst.at[part], send_sem=send.at[c], recv_sem=recv.at[c],
            device_id=(me, peer), device_id_type=MESH_ID)

    def to_inner(c):
        return hop(own, from_outer, a_send, a_recv, c, mate)

    def to_across(c):
        return hop(half, from_across, b_send, b_recv, c, across)

    def to_outer(c):
        return hop(whole, from_inner, c_send, c_recv, c, mate)

    def put(c, v):
        l = LD - MO - 1 - c // PIECES
        v = v.astype(f32)
        start = c % PIECES * PIECE
        full = min(max(3 * CH - start, 0), PIECE)
        if full:
            grads[l, 0, start:start + full] = v[:full, :CH]
            grads[l, 1, start:start + full] = v[:full, CH:]
        if full < PIECE:
            low = start + full - 3 * CH
            grads[l, 2, low:low + PIECE - full] = v[full:, :CH]
            low = low + 3 * CH // 2
            grads[l, 2, low:low + PIECE - full] = v[full:, CH:]

    def pair_sum(c):
        part = (c // PIECES, pl.ds(c % PIECES * PIECE, PIECE))
        to_inner(c).wait_recv()
        half[part] = (own[part].astype(f32) + from_outer[part].astype(f32)).astype(bf16)
        to_across(c).start()

    def full_sum(c):
        part = (c // PIECES, pl.ds(c % PIECES * PIECE, PIECE))
        to_across(c).wait_recv()
        v = (half[part].astype(f32) + from_across[part].astype(f32)).astype(bf16)
        whole[part] = v
        to_outer(c).start()
        put(c, v)

    def replicated(q, i):
        l = LD - 1 - i
        pair = (2 * q, 2 * q + 1)
        if i == 0:
            e = jnp.concatenate([adjs[s] for s in pair], axis=1).astype(f32)
        else:
            e = rep[...]
        h = jnp.tanh(jnp.concatenate([far[s, i, n] for s in pair for n in range(samples)], axis=1).astype(f32))
        v = cols(e)
        if i < MI - 1:
            rep[...] = e + STEP * (1.0 - h * h) * conv(weights[l], v)
        h = h.astype(bf16).astype(f32)
        h = jnp.concatenate([rows_down(h).astype(bf16), h.astype(bf16), rows_up(h).astype(bf16)], axis=0)
        return lax.dot_general(v, h, (((1,), (1,)), ((), ())), preferred_element_type=f32) * scale

    def packed(t):
        low = jnp.concatenate([t[:3 * CH // 2, 2 * CH:], t[3 * CH // 2:, 2 * CH:]], axis=1)
        return jnp.concatenate([t[:, :2 * CH], low], axis=0).astype(bf16)

    ps = [p[:, n * CELLS:(n + 1) * CELLS] for n in range(samples)]
    for i in range(LD):
        l = LD - 1 - i
        vs = [cols(q) for q in ps]
        ps = step(ps, vs, l)
        if i >= MI:
            v = jnp.concatenate(vs, axis=1)
            t = lax.dot_general(v, act_rows[l], (((1,), (1,)), ((), ())), preferred_element_type=f32) * scale
            own[i - MO] = packed(t)

            @pl.when(outer)
            def _():
                for c in range((i - MO) * PIECES, (i - MO + 1) * PIECES):
                    to_inner(c).start()
    for n in range(samples):
        bottoms[0, n] = ps[n]

    adj_copy(mate, 0, mate).wait_recv()

    @pl.when(inner)
    def _():
        adj_forwards()[0].start()
        adj_copy(across, 0, mate).wait_recv()
        adj_forwards()[1].start()

    pass_on(len(forwards))
    for i in range(MO):
        far_arrival(mate, i).wait_recv()

    @pl.when(inner)
    def _():
        for i in range(MO, MI):
            for j in range(1, parts):
                far_arrival(lax.rem(dp + j, parts), i).wait_recv()

    def sums(u):
        if summed + u < chunks:
            pair_sum(summed + u)
        if u >= LAG and summed + u - LAG < chunks:
            full_sum(summed + u - LAG)

    def accumulate(half_, i):
        l = LD - 1 - i
        t = replicated(near if half_ == 0 else 1 - near, i)
        gs = [t[:, a * CH:(a + 1) * CH] for a in range(3)]
        if half_ == 1:
            gs = [grads[l, a] + gs[a] for a in range(3)]
        if half_ == 1 and i >= MO:
            g = i - MO
            v = packed(jnp.concatenate(gs, axis=1))
            whole[g] = v
            for c in range(g * PIECES, (g + 1) * PIECES):
                to_outer(c).start()
                start = c % PIECES * PIECE
                put(c, v[start:start + PIECE])
        else:
            for a in range(3):
                grads[l, a] = gs[a]

    def units(half_):
        for i in range(MO):
            accumulate(half_, i)
        if MI > MO:
            @pl.when(inner)
            def _():
                for i in range(MO, MI):
                    accumulate(half_, i)

    units(0)

    @pl.when(inner)
    def _():
        for u in range(chunks - summed + LAG):
            sums(u)
            if u == FWD:
                adj_copy(3 - mate, 0, mate).wait_recv()
                adj_forwards()[2].start()

    @pl.when(outer)
    def _():
        for s in (2 - 2 * near, 3 - 2 * near):
            adj_copy(s, 0, mate).wait_recv()
            for i in range(MO):
                far_arrival(s, i).wait_recv()

    units(1)

    @pl.when(inner)
    def _():
        for c in range(chunks):
            if c >= summed:
                to_across(c).wait_send()
            to_outer(c).wait_send()
        adj_to_across().wait_send()
        for copy in adj_forwards():
            copy.wait_send()
        for n in (2, 3):
            for i in range(MO):
                far_forward(i, n).wait_send()

    @pl.when(outer)
    def _():
        for c in range(chunks):
            to_outer(c).wait_recv()
            part = (c // PIECES, pl.ds(c % PIECES * PIECE, PIECE))
            put(c, from_inner[part])
        for c in range(summed, chunks):
            to_inner(c).wait_send()

    adj_to_mate().wait_send()
    for i in range(MI):
        to_near, to_mate = far_sends(i)
        to_near.wait_send()
        if i < MO:
            to_mate.wait_send()
        else:
            @pl.when(outer)
            def _():
                to_mate.wait_send()

    for lower in range(0, blocks - 2, 2):
        @pl.when(jnp.logical_and(base > lower, me < blocks - 1))
        def _():
            mean_copy(lower + core).wait_send()

    @pl.when(jnp.logical_and(core == 1, me < blocks - 1))
    def _():
        mean_copy(me - 1).wait_send()

    for j in range(2, blocks - 1):
        @pl.when(jnp.logical_and(base + 1 < j, core == j % 2))
        def _():
            forward(j).wait_send()

    for peer in range(blocks - 2):
        @pl.when(base > peer)
        def _():
            src_copy(peer, peer % 2).wait_send()

    @pl.when(core == 1)
    def _():
        src_copy(me - 1, 0).wait_send()

    @pl.when(jnp.logical_or(jnp.logical_not(last), core == 1))
    def _():
        swap.wait_send()


def write(corrected, bottoms, grads, corrected_out, bottoms_out, grads_out, sem):
    stores = [pltpu.make_async_copy(grads, grads_out, sem.at[0]),
              pltpu.make_async_copy(corrected, corrected_out, sem.at[1]),
              pltpu.make_async_copy(bottoms, bottoms_out, sem.at[2])]
    for store in stores:
        store.start()
    for store in stores:
        store.wait()


def body(blocks, parts, states, kernels, boundary):
    samples = states.shape[1]
    lanes = samples * CELLS
    chunks = (LD - MO) * PIECES
    vmem = pl.BlockSpec(memory_space=pltpu.VMEM)
    hbm = pl.BlockSpec(memory_space=pltpu.HBM)
    dma = pltpu.SemaphoreType.DMA
    corrected, bottoms, grads = pl.pallas_call(
        functools.partial(kernel, blocks, parts, samples),
        out_shape=(
            jax.ShapeDtypeStruct(boundary.shape, f32),
            jax.ShapeDtypeStruct(boundary.shape, f32),
            jax.ShapeDtypeStruct((LD, 3, 3 * CH, CH), f32),
        ),
        in_specs=[hbm] * 3,
        out_specs=(vmem,) * 3,
        scratch_shapes=[
            pltpu.VMEM(states.shape, bf16),
            pltpu.VMEM((LD, 3, 3 * CH, CH), bf16),
            pltpu.VMEM(boundary.shape, f32),
            dma((3,)),
            pltpu.VMEM((blocks, 3 * CH, 3 * CH), bf16),
            pltpu.VMEM((LD, 3 * CH, 3 * CH), bf16),
            pltpu.VMEM((LD, CH, lanes), f32),
            pltpu.VMEM((LD, CH, lanes), bf16),
            pltpu.VMEM((LD - MI, 3 * CH, lanes), bf16),
            pltpu.VMEM((9 * CH // 2, 2 * CH), bf16),
            pltpu.VMEM((blocks, 9 * CH // 2, 2 * CH), bf16),
            pltpu.VMEM((2, CH, lanes // 2), bf16),
            pltpu.VMEM((blocks, CH, lanes // 2), bf16),
            pltpu.VMEM((CH, lanes), f32),
            *[pltpu.VMEM((CH, lanes // 2), f32)] * 3,
            pltpu.VMEM((parts, MI, samples, CH, CELLS), bf16),
            pltpu.VMEM((parts, CH, lanes), bf16),
            pltpu.VMEM((CH, 2 * lanes), f32),
            *[pltpu.VMEM((LD - MO, PACKED, 2 * CH), bf16)] * 6,
            dma((4, MI)), dma((parts, MI)), dma((5,)), dma((parts,)),
            *[dma((blocks,))] * 5, dma, dma,
            *[dma((chunks,))] * 6,
        ],
        compiler_params=pltpu.CompilerParams(
            collective_id=0, has_side_effects=True, vmem_limit_bytes=40 * 1024 * 1024),
        cost_estimate=pl.CostEstimate(flops=2 * 10**9, bytes_accessed=6 * 10**6, transcendentals=262144),
        name="cycle",
    )(*[pltpu.with_memory_space_constraint(a, pltpu.HBM) for a in (states, kernels.reshape(LD, 3, 3 * CH, CH), boundary)])
    shapes = (corrected, bottoms, grads)
    corrected, bottoms, grads = pl.pallas_call(
        write,
        out_shape=tuple(jax.ShapeDtypeStruct(a.shape, a.dtype) for a in shapes),
        in_specs=[pl.BlockSpec(memory_space=pl.ANY)] * 3,
        out_specs=(hbm,) * 3,
        scratch_shapes=[dma((3,))],
        cost_estimate=pl.CostEstimate(flops=0, bytes_accessed=5 * 10**6, transcendentals=0),
        compiler_params=pltpu.CompilerParams(vmem_limit_bytes=4 * 1024 * 1024),
        name="write",
    )(*[pltpu.with_memory_space_constraint(a, pltpu.VMEM) for a in shapes])
    return corrected, bottoms, grads.reshape(LD, 9, CH, CH)


def solution(mesh):
    placed = (
        P("layer", "dp", None, None),
        P("layer", None, None, None),
        P("layer", "dp", None, None),
    )
    return jax.shard_map(
        functools.partial(body, mesh.shape["layer"], mesh.shape["dp"]),
        mesh=mesh,
        in_specs=placed,
        out_specs=(
            P("layer", "dp", None, None),
            P("layer", "dp", None, None),
            P("layer", None, None, None),
        ),
        check_vma=False,
    )
```
